32 devices in a mesh: ctx: 4 (over y, core), pb: 8 (over z, x).
Axes of the slice: x: 2, y: 2, z: 4, core: 2. Of those that a mesh axis runs over, the one named last changes fastest.
Arguments:
- queries: bfloat16 [128, 64, 8, 128], P('pb'), may hold values from -6 to 6
- keys: bfloat16 [4096, 128], P('ctx'), may hold values from -6 to 6
- values: bfloat16 [4096, 128], P('ctx'), may hold values from -6 to 6
- outputs_saved: bfloat16 [128, 64, 8, 128], P('pb'), may hold values from -6 to 6
- grad_out: bfloat16 [128, 64, 8, 128], P('pb'), may hold values from -6 to 6
- saved_lse: float32 [128, 64, 8], P('pb'), may hold values from 7 to 9
- block_lists: int32 [128, 24], P('pb'), may hold values from -1 to 31, as said below
Outputs:
- query_grad: float32 [128, 64, 8, 128], P('pb', 'ctx')
- key_grad: float32 [4096, 128], P(('ctx', 'pb'))
- value_grad: float32 [4096, 128], P(('ctx', 'pb'))
The draws below stay inside these ranges and needn't reach their ends.
Inputs may be any that keep to these rules, and one draw needn't show every extreme that they name: `block_lists`: each row lists distinct blocks in rising order, then -1 in the remaining entries. Of one row's blocks at most 6 lie in one run of 8 blocks (j * 8 to j * 8 + 7), and in every row exactly 6 lie in some such run.
All inputs are finite; a program needn't handle non-finite values.
Results may differ from the reference program's by a relative error of at most 0.0029.
Values sent between devices are 32-bit elements; how exact they have to be, the bound alone decides.
No kernel may reach another device: no remote copies, remote signals or barrier semaphores. Data moves between devices by JAX's collectives and lax.ppermute only.
A program may use at most 128 MiB of HBM per device.

```python
import jax
import jax.numpy as jnp
from jax import lax

D_HEAD = 128
HEADS = 8
QLEN = 64
BLK = 128
CAP = 6
BLK_DEV = 8
QUESTIONS = 128
NB = 32
KEYS = 4096
LIST = 24


def draw_block_lists(key, part):
    shards = NB // BLK_DEV
    key_popular, key_count, key_hot, key_rank = jax.random.split(key, 4)
    popularity = jax.random.randint(key_popular, (1, shards), CAP // 2, CAP + 1)
    counts_shard = jax.random.randint(key_count, (QUESTIONS, shards), 0, popularity + 1)
    hot_shard = jax.random.randint(key_hot, (QUESTIONS, 1), 0, shards)
    counts_shard = jnp.where(jnp.arange(shards)[None, :] == hot_shard, CAP, counts_shard)
    raw_scores = jax.random.randint(key_rank, (QUESTIONS, shards, BLK_DEV), 0, 1 << 20)
    raw_scores = raw_scores * BLK_DEV + jnp.arange(BLK_DEV, dtype=jnp.int32)[None, None, :]
    rank_in = jnp.argsort(jnp.argsort(-raw_scores, axis=2, stable=True), axis=2, stable=True)
    member = (rank_in < counts_shard[:, :, None]).reshape(QUESTIONS, NB)
    block_ids = jnp.arange(NB, dtype=jnp.int32)[None, :]
    sort_score = jnp.where(member, 2 * NB - block_ids, NB - 1 - block_ids)
    top_values, top_index = jax.lax.top_k(sort_score, LIST)
    return jnp.where(top_values > NB, 2 * NB - top_values, -1).astype(jnp.int32)


def shard_levels(stream_key, dims, cuts, least, largest):
    factor_of = 1.0
    for position, parts in cuts:
        draws = jax.random.uniform(jax.random.fold_in(jax.random.fold_in(stream_key, 6), position), (parts,), jnp.float32, least / len(cuts), largest / len(cuts))
        factor_of = factor_of * jnp.repeat(jnp.exp(draws), dims[position] // parts).reshape((-1,) + (1,) * (len(dims) - 1 - position))
    return factor_of


def gaussian(rng, extent, spread, limit, pieces=(), kind=jnp.bfloat16):
    gain = shard_levels(rng, extent, pieces, -0.22, 0.18) if pieces else 1.0
    array = jax.random.normal(rng, extent, jnp.float32) * spread * gain
    return jnp.minimum(jnp.maximum(array, -limit), limit).astype(kind)


def setup_inputs(seed: int = 0) -> dict:
    splits = jax.random.split(jax.random.key(seed), 8)
    queries = gaussian(splits[0], (QUESTIONS, QLEN, HEADS, D_HEAD), 1.0, 6.0, ((0, 8),))
    keys = gaussian(splits[1], (KEYS, D_HEAD), 1.0, 6.0, ((0, 4),))
    values = gaussian(splits[2], (KEYS, D_HEAD), 1.0, 6.0, ((0, 4),))
    outputs_saved = gaussian(splits[3], (QUESTIONS, QLEN, HEADS, D_HEAD), 1.0, 6.0, ((0, 8),))
    grad_out = gaussian(splits[4], (QUESTIONS, QLEN, HEADS, D_HEAD), 1.0, 6.0, ((0, 8),))
    saved_lse = jnp.clip(7.0 + 2.0 * jax.random.uniform(splits[5], (QUESTIONS, QLEN, HEADS), jnp.float32) ** shard_levels(splits[5], (QUESTIONS, QLEN, HEADS), ((0, 8),), -0.2, 0.2), 7.0, 9.0)
    block_lists = draw_block_lists(jax.random.fold_in(splits[7], 71), 0)
    return {"queries": queries, "keys": keys, "values": values, "outputs_saved": outputs_saved, "grad_out": grad_out, "saved_lse": saved_lse, "block_lists": block_lists}


def reference(queries, keys, values, outputs_saved, grad_out, saved_lse, block_lists):
    factor = D_HEAD ** -0.5
    key_blocks = keys.reshape(NB, BLK, D_HEAD)
    value_blocks = values.reshape(NB, BLK, D_HEAD)
    row_delta = jnp.sum(grad_out.astype(jnp.float32) * outputs_saved.astype(jnp.float32), axis=-1)

    def question_step(totals, element):
        key_acc, value_acc = totals
        q_all, dout_all, lse_all, delta_all, listing = element
        live_slots = listing >= 0
        chosen = jnp.where(live_slots, listing, 0).astype(jnp.int32)
        key_slab = key_blocks[chosen].reshape(LIST * BLK, D_HEAD).astype(jnp.float32)
        value_slab = value_blocks[chosen].reshape(LIST * BLK, D_HEAD).astype(jnp.float32)
        live_cols = jnp.repeat(live_slots, BLK)
        q_rows = q_all.reshape(QLEN * HEADS, D_HEAD).astype(jnp.float32)
        dout_rows = dout_all.reshape(QLEN * HEADS, D_HEAD).astype(jnp.float32)
        scores = factor * jnp.dot(q_rows, key_slab.T, preferred_element_type=jnp.float32)
        prob_tile = jnp.where(live_cols[None, :], jnp.exp(scores - lse_all.reshape(-1)[:, None]), 0.0)
        dprob_tile = jnp.dot(dout_rows, value_slab.T, preferred_element_type=jnp.float32)
        dscore = (prob_tile * (dprob_tile - delta_all.reshape(-1)[:, None])).astype(jnp.bfloat16)
        prob_low = prob_tile.astype(jnp.bfloat16)
        dscore_wide = dscore.astype(jnp.float32)
        query_part = factor * jnp.dot(dscore_wide, key_slab, preferred_element_type=jnp.float32)
        key_part = factor * jnp.dot(dscore_wide.T, q_rows, preferred_element_type=jnp.float32)
        value_part = jnp.dot(prob_low.astype(jnp.float32).T, dout_rows, preferred_element_type=jnp.float32)
        weight_live = live_slots.astype(key_part.dtype)[:, None, None]
        key_acc = key_acc.at[chosen].add(key_part.reshape(LIST, BLK, D_HEAD) * weight_live)
        value_acc = value_acc.at[chosen].add(value_part.reshape(LIST, BLK, D_HEAD) * weight_live)
        return (key_acc, value_acc), query_part.reshape(QLEN, HEADS, D_HEAD)

    zero_acc = jnp.zeros((NB, BLK, D_HEAD), jnp.float32)
    (key_acc, value_acc), query_grad = lax.scan(
        question_step, (zero_acc, zero_acc), (queries, grad_out, saved_lse, row_delta, block_lists))
    return query_grad, key_acc.reshape(KEYS, D_HEAD), value_acc.reshape(KEYS, D_HEAD)
```

```python
from functools import partial
import math

import jax
import jax.numpy as jnp
from jax import lax
from jax.experimental import pallas as pl
from jax.experimental.pallas import tpu as pltpu
from jax.sharding import PartitionSpec as P

BLK = 128
BLK_DEV = 8

NN = (((1,), (0,)), ((), ()))
NT = (((1,), (1,)), ((), ()))


def mm(a, b, dims):
    return lax.dot_general(a, b, dims, preferred_element_type=jnp.float32)


def backward_kernel(
    first_question,
    factor,
    lists,
    place,
    q_ref,
    o_ref,
    do_ref,
    lse_ref,
    k_ref,
    v_ref,
    dq_ref,
    dk_ref,
    dv_ref,
    dk_acc,
    dv_acc,
    kt,
    dqt,
    dq_rows,
):
    step = pl.program_id(0)
    question = step + first_question
    width = k_ref.shape[-1]
    ctx_me, pb_me = place[0], place[1]

    @pl.when(step == 0)
    def _():
        dk_acc[...] = jnp.zeros_like(dk_acc)
        dv_acc[...] = jnp.zeros_like(dv_acc)
        for b in range(BLK_DEV):
            kt[b] = k_ref[b].T

    first_block = ctx_me * BLK_DEV
    start = jnp.int32(0)
    stop = jnp.int32(0)
    for entry in range(lists.shape[1]):
        block = lists[question, entry]
        start += jnp.where((block >= 0) & (block < first_block), 1, 0)
        stop += jnp.where((block >= 0) & (block < first_block + BLK_DEV), 1, 0)
    count = stop - start

    q = q_ref[0]
    do = do_ref[0]
    product = do.astype(jnp.float32) * o_ref[0].astype(jnp.float32)
    high = product.astype(jnp.bfloat16)
    low = (product - high.astype(jnp.float32)).astype(jnp.bfloat16)
    ones = jnp.ones((8, width), jnp.bfloat16)
    delta = (mm(ones, high, NT) + mm(ones, low, NT))[0:1]
    lse = lse_ref[0] * math.log2(math.e)
    scale = factor * math.log2(math.e)
    dqt[...] = jnp.zeros_like(dqt)

    def tiles(blocks):
        keys = jnp.concatenate([k_ref[b] for b in blocks], axis=0)
        values = jnp.concatenate([v_ref[b] for b in blocks], axis=0)
        keys_t = jnp.concatenate([kt[b] for b in blocks], axis=1)
        prob = jnp.exp2(mm(keys, q, NT) * scale - lse)
        dscore = (prob * (mm(values, do, NT) - delta)).astype(jnp.bfloat16)
        dv = mm(prob.astype(jnp.bfloat16), do, NN)
        dk = mm(dscore, q, NN)
        dqt[...] += mm(keys_t, dscore, NN)
        for i, b in enumerate(blocks):
            dv_acc[b] += dv[i * BLK : (i + 1) * BLK]
            dk_acc[b] += dk[i * BLK : (i + 1) * BLK]

    def pair(i, carry):
        at = start + 2 * i
        tiles([lists[question, at] - first_block, lists[question, at + 1] - first_block])
        return carry

    lax.fori_loop(0, count // 2, pair, 0)

    @pl.when(count % 2 == 1)
    def _():
        tiles([lists[question, stop - 1] - first_block])

    dq_rows[...] = dqt[...].T * factor
    parts, rows = dq_ref.shape[0], dq_ref.shape[2]
    for j in range(parts):
        at = pl.multiple_of((ctx_me ^ j) * rows, rows)
        dq_ref[j, 0] = dq_rows[pl.ds(at, rows)]

    @pl.when(step == pl.num_programs(0) - 1)
    def _():
        parts, rows = dk_ref.shape[0], dk_ref.shape[1]
        per = BLK // rows
        for j in range(parts):
            dest = pb_me ^ j
            at = pl.multiple_of((dest % per) * rows, rows)
            dk_ref[j] = dk_acc[dest // per, pl.ds(at, rows)] * factor
            dv_ref[j] = dv_acc[dest // per, pl.ds(at, rows)]


def backward(lists, place, queries, outputs, grads, lse, keys, values, ctx_size, pb_size, first_question, count):
    _, rows, width = queries.shape
    factor = width ** (-0.5)
    local_keys = keys.shape[0] * keys.shape[1]
    per_question = lambda i, *_: (i + first_question, 0, 0)
    whole = lambda i, *_: (0, 0, 0)
    question_spec = pl.BlockSpec((1, rows, width), per_question)
    key_spec = pl.BlockSpec(keys.shape, whole)
    grad_shape = (pb_size, local_keys // pb_size, width)
    dq_shape = (ctx_size, count, rows // ctx_size, width)
    return pl.pallas_call(
        partial(backward_kernel, first_question, factor),
        grid_spec=pltpu.PrefetchScalarGridSpec(
            num_scalar_prefetch=2,
            grid=(count,),
            in_specs=[
                question_spec,
                question_spec,
                question_spec,
                pl.BlockSpec((1, 1, rows), per_question),
                key_spec,
                key_spec,
            ],
            out_specs=[
                pl.BlockSpec((ctx_size, 1, rows // ctx_size, width), lambda i, *_: (0, i, 0, 0)),
                pl.BlockSpec(grad_shape, whole),
                pl.BlockSpec(grad_shape, whole),
            ],
            scratch_shapes=[
                pltpu.VMEM(keys.shape, jnp.float32),
                pltpu.VMEM(keys.shape, jnp.float32),
                pltpu.VMEM((keys.shape[0], width, BLK), jnp.bfloat16),
                pltpu.VMEM((width, rows), jnp.float32),
                pltpu.VMEM((rows, width), jnp.float32),
            ],
        ),
        out_shape=[
            jax.ShapeDtypeStruct(dq_shape, jnp.float32),
            jax.ShapeDtypeStruct(grad_shape, jnp.float32),
            jax.ShapeDtypeStruct(grad_shape, jnp.float32),
        ],
        compiler_params=pltpu.CompilerParams(vmem_limit_bytes=40 * 1024 * 1024),
        cost_estimate=pl.CostEstimate(
            flops=count * rows * local_keys * width * 5, bytes_accessed=count * rows * width * 12, transcendentals=0
        ),
        name="attention_backward",
    )(lists, place, queries, outputs, grads, lse, keys, values)


def swap(array, axis, size, bit):
    return lax.ppermute(array, axis, [(i, i ^ bit) for i in range(size)])


def halving(parts, axis, size, bits):
    for bit in bits:
        kept = [j for j in parts if not j & bit]
        sent = swap(jnp.stack([parts[j | bit] for j in kept]), axis, size, bit)
        parts = {j: parts[j] + sent[i] for i, j in enumerate(kept)}
    return parts[0]


def local(ctx_size, pb_size, queries, keys, values, outputs_saved, grad_out, saved_lse, block_lists):
    questions, tokens, heads, width = queries.shape
    rows = tokens * heads
    flat = lambda a: a.reshape(questions, rows, width)
    blocked = lambda a: a.reshape(BLK_DEV, BLK, width)
    place = jnp.stack([lax.axis_index("ctx"), lax.axis_index("pb")]).astype(jnp.int32)
    dq, dk, dv = backward(
        block_lists,
        place,
        flat(queries),
        flat(outputs_saved),
        flat(grad_out),
        saved_lse.reshape(questions, 1, rows),
        blocked(keys),
        blocked(values),
        ctx_size,
        pb_size,
        0,
        questions,
    )
    ctx_bits = [1 << i for i in range(ctx_size.bit_length() - 1)]
    pb_bits = [1 << i for i in range(pb_size.bit_length() - 1)]
    query_grad = halving({j: dq[j] for j in range(ctx_size)}, "ctx", ctx_size, ctx_bits)
    both = jnp.concatenate([dk, dv], axis=1)
    both = halving({j: both[j] for j in range(pb_size)}, "pb", pb_size, pb_bits)
    half = both.shape[0] // 2
    return (
        query_grad.reshape(questions, tokens // ctx_size, heads, width),
        both[:half],
        both[half:],
    )


def solution(mesh):
    ctx_size, pb_size = mesh.shape["ctx"], mesh.shape["pb"]
    placed = (
        P("pb", None, None, None),
        P("ctx", None),
        P("ctx", None),
        P("pb", None, None, None),
        P("pb", None, None, None),
        P("pb", None, None),
        P("pb", None),
    )
    return jax.shard_map(
        partial(local, ctx_size, pb_size),
        mesh=mesh,
        in_specs=placed,
        out_specs=(P("pb", "ctx", None, None), P(("ctx", "pb"), None), P(("ctx", "pb"), None)),
        check_vma=False,
    )
```

```python
from functools import partial
import math

import jax
import jax.numpy as jnp
from jax import lax
from jax.experimental import pallas as pl
from jax.experimental.pallas import tpu as pltpu
from jax.sharding import PartitionSpec as P

BLK = 128
BLK_DEV = 8
PAIRS = BLK_DEV // 2
NONE = BLK_DEV

NN = (((1,), (0,)), ((), ()))
NT = (((1,), (1,)), ((), ()))
TN = (((0,), (0,)), ((), ()))


def mm(a, b, dims):
    return lax.dot_general(a, b, dims, preferred_element_type=jnp.float32)


def backward_kernel(first, count, factor, has_prior, has_after, *refs):
    lists_hbm, lse_hbm, q_hbm, o_hbm, do_hbm, k_hbm, v_hbm = refs[:7]
    refs = refs[7:]
    prior = refs[:2] if has_prior else None
    refs = refs[2:] if has_prior else refs
    refs = refs[1:] if has_after else refs
    dq_ref, dk_ref, dv_ref = refs[:3]
    q_all, o_all, do_all, k_all, v_all, lse_all, delta_all, dk_acc, dv_acc = refs[3:12]
    prob0, prob1, ds0, ds1, lse_ref, lists, items, sems = refs[12:]
    prob_slots, ds_slots = (prob0, prob1), (ds0, ds1)
    rows, width = q_all.shape[1], q_all.shape[2]
    ctx_me, pb_me = lax.axis_index("ctx"), lax.axis_index("pb")

    mine = pl.ds(first, count)
    copies = [
        pltpu.make_async_copy(src, dst, sems.at[n])
        for n, (src, dst) in enumerate(
            (
                (lists_hbm, lists),
                (lse_hbm.at[mine], lse_ref),
                (do_hbm.at[mine], do_all),
                (o_hbm.at[mine], o_all),
                (q_hbm.at[mine], q_all),
                (k_hbm, k_all.at[pl.ds(0, BLK_DEV)]),
                (v_hbm, v_all.at[pl.ds(0, BLK_DEV)]),
            )
        )
    ]
    for copy in copies:
        copy.start()

    dq_ref[...] = jnp.zeros_like(dq_ref)
    dk_acc[...] = jnp.zeros_like(dk_acc)
    dv_acc[...] = jnp.zeros_like(dv_acc)
    k_all[NONE] = jnp.zeros((BLK, width), k_all.dtype)
    v_all[NONE] = jnp.zeros((BLK, width), v_all.dtype)

    copies[0].wait()
    first_block = ctx_me * BLK_DEV
    below, above = first_block.astype(jnp.uint32), (first_block + BLK_DEV).astype(jnp.uint32)
    last = lists.shape[1] - 1
    total = jnp.int32(0)
    for i in range(count):
        start = jnp.int32(0)
        stop = jnp.int32(0)
        for entry in range(last + 1):
            block = lists[first + i, entry].astype(jnp.uint32)
            start += (block < below).astype(jnp.int32)
            stop += (block < above).astype(jnp.int32)
        for p in range(PAIRS):
            at = start + 2 * p
            items[0, total + p] = i
            items[1, total + p] = lists[first + i, jnp.minimum(at, last)] - first_block
            items[2, total + p] = jnp.where(
                at + 1 < stop, lists[first + i, jnp.minimum(at + 1, last)] - first_block, NONE
            )
        total += (stop - start + 1) // 2
    for p in range(2):
        items[0, total + p] = 0
        items[1, total + p] = NONE
        items[2, total + p] = NONE

    copies[1].wait()
    heads, tokens = lse_ref.shape[1], lse_ref.shape[2]
    lse_rest = lse_ref[...].reshape(count * heads, tokens) * math.log2(math.e)
    row = lax.broadcasted_iota(jnp.int32, (tokens, rows), 1) // heads
    spread = (row == lax.broadcasted_iota(jnp.int32, (tokens, rows), 0)).astype(jnp.bfloat16)
    lse_rows = jnp.zeros((count * heads, rows), jnp.float32)
    for _ in range(3):
        piece = lse_rest.astype(jnp.bfloat16)
        lse_rest = lse_rest - piece.astype(jnp.float32)
        lse_rows += mm(piece, spread, NN)
    head_of_row = lax.broadcasted_iota(jnp.int32, (heads, rows), 1) % heads
    own_head = head_of_row == lax.broadcasted_iota(jnp.int32, (heads, rows), 0)
    for i in range(count):
        picked = jnp.where(own_head, lse_rows[i * heads : (i + 1) * heads], 0.0)
        lse_all[i] = jnp.sum(picked, axis=0, keepdims=True)

    for copy in copies[2:]:
        copy.wait()
    ones = jnp.ones((8, 2 * width), jnp.bfloat16)
    for i in range(count):
        product = do_all[i].astype(jnp.float32) * o_all[i].astype(jnp.float32)
        high = product.astype(jnp.bfloat16)
        low = (product - high.astype(jnp.float32)).astype(jnp.bfloat16)
        delta_all[i] = mm(ones, jnp.concatenate([high, low], axis=1), NT)[0:1]

    scale = factor * math.log2(math.e)
    parts, part_rows = dq_ref.shape[0], dq_ref.shape[2]

    def scores(item, slot):
        i, b0, b1 = items[0, item], items[1, item], items[2, item]
        keys = jnp.concatenate([k_all[b0], k_all[b1]], axis=0)
        values = jnp.concatenate([v_all[b0], v_all[b1]], axis=0)
        prob = jnp.exp2(mm(keys, q_all[i], NT) * scale - lse_all[i])
        dprob = mm(values, do_all[i], NT)
        prob_slots[slot][...] = prob.astype(jnp.bfloat16)
        ds_slots[slot][...] = (prob * (dprob - delta_all[i])).astype(jnp.bfloat16)

    def gradients(item, slot):
        i, b0, b1 = items[0, item], items[1, item], items[2, item]
        keys = jnp.concatenate([k_all[b0], k_all[b1]], axis=0)
        dscore = ds_slots[slot][...]
        dv = mm(prob_slots[slot][...], do_all[i], NN)
        dk = mm(dscore, q_all[i], NN)
        dq = mm(dscore, keys, TN) * factor
        for j in range(parts):
            dq_ref[ctx_me ^ j, i] += dq[j * part_rows : (j + 1) * part_rows]
        dv_acc[b0] += dv[:BLK]
        dk_acc[b0] += dk[:BLK]
        dv_acc[b1] += dv[BLK:]
        dk_acc[b1] += dk[BLK:]

    scores(0, 0)

    def two_items(step, carry):
        scores(2 * step + 1, 1)
        gradients(2 * step, 0)
        scores(2 * step + 2, 0)
        gradients(2 * step + 1, 1)
        return carry

    lax.fori_loop(0, (total + 1) // 2, two_items, 0)

    parts, part_rows = dk_ref.shape[0], dk_ref.shape[1]
    per = BLK // part_rows
    for j in range(parts):
        dest = pb_me ^ j
        at = pl.multiple_of((dest % per) * part_rows, part_rows)
        dk = dk_acc[dest // per, pl.ds(at, part_rows)] * factor
        dv = dv_acc[dest // per, pl.ds(at, part_rows)]
        dk_ref[j] = dk + prior[0][j] if has_prior else dk
        dv_ref[j] = dv + prior[1][j] if has_prior else dv


def backward(lists, lse, queries, outputs, grads, keys, values, sizes, first, count, prior=(), after=()):
    ctx_size, pb_size = sizes
    _, rows, width = queries.shape
    heads = lse.shape[1]
    local_keys = keys.shape[0] * keys.shape[1]
    grad_shape = (pb_size, local_keys // pb_size, width)
    dq_shape = (ctx_size, count, rows // ctx_size, width)
    vmem = pl.BlockSpec(memory_space=pltpu.VMEM)
    hbm = pl.BlockSpec(memory_space=pltpu.HBM)
    f32, bf16 = jnp.float32, jnp.bfloat16
    in_hbm = [pltpu.with_memory_space_constraint(a, pltpu.HBM) for a in (lists, lse, queries, outputs, grads, keys, values)]
    return pl.pallas_call(
        partial(backward_kernel, first, count, width ** (-0.5), bool(prior), bool(after)),
        in_specs=[hbm] * 7 + [vmem] * len(prior) + [pl.BlockSpec(memory_space=pl.ANY)] * len(after),
        out_specs=[vmem] * 3,
        out_shape=[
            pltpu.VMEM(dq_shape, f32),
            pltpu.VMEM(grad_shape, f32),
            pltpu.VMEM(grad_shape, f32),
        ],
        scratch_shapes=[
            pltpu.VMEM((count, rows, width), bf16),
            pltpu.VMEM((count, rows, width), bf16),
            pltpu.VMEM((count, rows, width), bf16),
            pltpu.VMEM((BLK_DEV + 1, BLK, width), bf16),
            pltpu.VMEM((BLK_DEV + 1, BLK, width), bf16),
            pltpu.VMEM((count, 1, rows), f32),
            pltpu.VMEM((count, 1, rows), f32),
            pltpu.VMEM((BLK_DEV + 1, BLK, width), f32),
            pltpu.VMEM((BLK_DEV + 1, BLK, width), f32),
            pltpu.VMEM((2 * BLK, rows), bf16),
            pltpu.VMEM((2 * BLK, rows), bf16),
            pltpu.VMEM((2 * BLK, rows), bf16),
            pltpu.VMEM((2 * BLK, rows), bf16),
            pltpu.VMEM((count,) + lse.shape[1:], f32),
            pltpu.SMEM(lists.shape, jnp.int32),
            pltpu.SMEM((3, (count + 1) * PAIRS), jnp.int32),
            pltpu.SemaphoreType.DMA((7,)),
        ],
        compiler_params=pltpu.CompilerParams(vmem_limit_bytes=32 * 1024 * 1024),
        cost_estimate=pl.CostEstimate(
            flops=count * rows * local_keys * width * 5, bytes_accessed=count * rows * width * 12, transcendentals=0
        ),
        name="attention_backward",
    )(*in_hbm, *prior, *after)


def swap(array, axis, size, bit):
    return lax.ppermute(array, axis, [(i, i ^ bit) for i in range(size)])


def exchange(groups, axis, size, bit):
    sent = jnp.stack([parts[j] for parts in groups for j in sorted(parts) if j & bit])
    got = iter(swap(sent, axis, size, bit))
    return [{j: parts[j] + next(got) for j in sorted(parts) if not j & bit} for parts in groups]


def bits_of(size):
    return [1 << i for i in range(size.bit_length() - 1)]


def sum_two_ways(first, second, axis, size, after):
    order = bits_of(size)
    other = order[1::-1] + order[2:]
    for one, two in zip(order, other):
        if one == two:
            first, second = exchange([first, second], axis, size, one)
        else:
            (first,) = exchange([first], axis, size, one)
            (second,) = exchange([second], axis, size, two)
    return first[0], second[0]


def local(ctx_size, pb_size, queries, keys, values, outputs_saved, grad_out, saved_lse, block_lists):
    questions, tokens, heads, width = queries.shape
    rows = tokens * heads
    flat = lambda a: a.reshape(questions, rows, width)
    blocked = lambda a: a.reshape(BLK_DEV, BLK, width)
    run = partial(
        backward,
        block_lists,
        jnp.swapaxes(saved_lse, 1, 2),
        flat(queries),
        flat(outputs_saved),
        flat(grad_out),
        blocked(keys),
        blocked(values),
        (ctx_size, pb_size),
    )
    early = questions * 9 // 16
    core, rest = bits_of(ctx_size)[0], bits_of(ctx_size)[1:]
    by_dest = lambda a: {j: a[j] for j in range(a.shape[0])}

    def across(parts):
        for bit in rest:
            (parts,) = exchange([parts], "ctx", ctx_size, bit)
        return parts[0]

    dq, dk, dv = run(0, early)
    (parts,) = exchange([by_dest(dq)], "ctx", ctx_size, core)
    early_grad = across(parts)
    dq, dk, dv = run(early, questions - early, (dk, dv), (parts[2],))
    dq, early_grad = lax.optimization_barrier((dq, early_grad))
    (parts,) = exchange([by_dest(dq)], "ctx", ctx_size, core)
    key_grad, value_grad = sum_two_ways(by_dest(dk), by_dest(dv), "pb", pb_size, parts)
    mine, key_grad, value_grad = lax.optimization_barrier((parts[0], key_grad, value_grad))
    parts = {**parts, 0: mine}
    late_grad = across(parts)
    done = [early_grad, late_grad]
    query_grad = jnp.concatenate(done, axis=0)
    return query_grad.reshape(questions, tokens // ctx_size, heads, width), key_grad, value_grad


def solution(mesh):
    ctx_size, pb_size = mesh.shape["ctx"], mesh.shape["pb"]
    placed = (
        P("pb", None, None, None),
        P("ctx", None),
        P("ctx", None),
        P("pb", None, None, None),
        P("pb", None, None, None),
        P("pb", None, None),
        P("pb", None),
    )
    return jax.shard_map(
        partial(local, ctx_size, pb_size),
        mesh=mesh,
        in_specs=placed,
        out_specs=(P("pb", "ctx", None, None), P(("ctx", "pb"), None), P(("ctx", "pb"), None)),
        check_vma=False,
    )
```

```python
from functools import partial
import math

import jax
import jax.numpy as jnp
from jax import lax
from jax.experimental import pallas as pl
from jax.experimental.pallas import tpu as pltpu
from jax.sharding import PartitionSpec as P

BLK = 128
BLK_DEV = 8
PAIRS = BLK_DEV // 2
NONE = BLK_DEV
CORE = 1

NN = (((1,), (0,)), ((), ()))
NT = (((1,), (1,)), ((), ()))
TN = (((0,), (0,)), ((), ()))


def mm(a, b, dims):
    return lax.dot_general(a, b, dims, preferred_element_type=jnp.float32)


def list_items(lists, items, questions, base):
    first_block = lax.axis_index("ctx") * BLK_DEV
    below, above = first_block.astype(jnp.uint32), (first_block + BLK_DEV).astype(jnp.uint32)
    last = lists.shape[1] - 1
    end = base
    for i in questions:
        start = jnp.int32(0)
        stop = jnp.int32(0)
        for entry in range(last + 1):
            block = lists[i, entry].astype(jnp.uint32)
            start += (block < below).astype(jnp.int32)
            stop += (block < above).astype(jnp.int32)
        for p in range(PAIRS):
            at = start + 2 * p
            items[0, end + p] = i
            items[1, end + p] = lists[i, jnp.minimum(at, last)] - first_block
            items[2, end + p] = jnp.where(at + 1 < stop, lists[i, jnp.minimum(at + 1, last)] - first_block, NONE)
        end += (stop - start + 1) // 2
    for p in range(2):
        items[0, end + p] = questions[0]
        items[1, end + p] = NONE
        items[2, end + p] = NONE
    return end


def spread_lse(lse, out, rows):
    count, heads, tokens = lse.shape
    rest = lse[...].reshape(count * heads, tokens) * math.log2(math.e)
    row = lax.broadcasted_iota(jnp.int32, (tokens, rows), 1) // heads
    spread = (row == lax.broadcasted_iota(jnp.int32, (tokens, rows), 0)).astype(jnp.bfloat16)
    wide = jnp.zeros((count * heads, rows), jnp.float32)
    for _ in range(3):
        piece = rest.astype(jnp.bfloat16)
        rest = rest - piece.astype(jnp.float32)
        wide += mm(piece, spread, NN)
    head_of_row = lax.broadcasted_iota(jnp.int32, (heads, rows), 1) % heads
    own_head = head_of_row == lax.broadcasted_iota(jnp.int32, (heads, rows), 0)
    for i in range(count):
        picked = jnp.where(own_head, wide[i * heads : (i + 1) * heads], 0.0)
        out[i] = jnp.sum(picked, axis=0, keepdims=True)


def backward_kernel(
    factor,
    lists_hbm, lse_hbm, q_hbm, o_hbm, do_hbm, k_hbm, v_hbm,
    dq_ref, dk_ref, dv_ref,
    q_all, o_all, do_all, k_all, v_all, lse_all, delta_all, dk_acc, dv_acc,
    prob0, prob1, ds0, ds1, lse, lists, items, sems,
):
    prob_slots, ds_slots = (prob0, prob1), (ds0, ds1)
    count, rows, width = q_all.shape
    ctx_me, pb_me = lax.axis_index("ctx"), lax.axis_index("pb")
    copies = [
        pltpu.make_async_copy(src, dst, sems.at[n])
        for n, (src, dst) in enumerate(
            [(lists_hbm, lists), (lse_hbm, lse), (do_hbm, do_all), (o_hbm, o_all), (q_hbm, q_all)]
            + [(src, dst.at[pl.ds(0, BLK_DEV)]) for src, dst in ((k_hbm, k_all), (v_hbm, v_all))]
        )
    ]
    for copy in copies:
        copy.start()

    dq_ref[...] = jnp.zeros_like(dq_ref)
    dk_acc[...] = jnp.zeros_like(dk_acc)
    dv_acc[...] = jnp.zeros_like(dv_acc)
    k_all[NONE] = jnp.zeros((BLK, width), k_all.dtype)
    v_all[NONE] = jnp.zeros((BLK, width), v_all.dtype)
    copies[0].wait()
    total = list_items(lists, items, range(count), jnp.int32(0))
    copies[1].wait()
    spread_lse(lse, lse_all, rows)
    scale = factor * math.log2(math.e)
    parts, part_rows = dq_ref.shape[0], dq_ref.shape[2]

    def row_deltas(questions):
        ones = jnp.ones((8, 2 * width), jnp.bfloat16)
        for i in questions:
            product = do_all[i].astype(jnp.float32) * o_all[i].astype(jnp.float32)
            high = product.astype(jnp.bfloat16)
            low = (product - high.astype(jnp.float32)).astype(jnp.bfloat16)
            delta_all[i] = mm(ones, jnp.concatenate([high, low], axis=1), NT)[0:1]

    def scores(item, slot):
        i, b0, b1 = items[0, item], items[1, item], items[2, item]
        keys = jnp.concatenate([k_all[b0], k_all[b1]], axis=0)
        values = jnp.concatenate([v_all[b0], v_all[b1]], axis=0)
        prob = jnp.exp2(mm(keys, q_all[i], NT) * scale - lse_all[i])
        dprob = mm(values, do_all[i], NT)
        prob_slots[slot][...] = prob.astype(jnp.bfloat16)
        ds_slots[slot][...] = (prob * (dprob - delta_all[i])).astype(jnp.bfloat16)

    def gradients(item, slot):
        i, b0, b1 = items[0, item], items[1, item], items[2, item]
        keys = jnp.concatenate([k_all[b0], k_all[b1]], axis=0)
        dscore = ds_slots[slot][...]
        dv = mm(prob_slots[slot][...], do_all[i], NN)
        dk = mm(dscore, q_all[i], NN)
        dq = mm(dscore, keys, TN) * factor
        for j in range(parts):
            dq_ref[ctx_me ^ j, i] += dq[j * part_rows : (j + 1) * part_rows]
        dv_acc[b0] += dv[:BLK]
        dk_acc[b0] += dk[:BLK]
        dv_acc[b1] += dv[BLK:]
        dk_acc[b1] += dk[BLK:]

    def sweep(base, total):
        def several(first, step_items):
            def body(step, carry):
                at = first + step_items * step
                for n in range(0, step_items, 2):
                    scores(at + n + 1, 1)
                    gradients(at + n, 0)
                    scores(at + n + 2, 0)
                    gradients(at + n + 1, 1)
                return carry

            return body

        scores(base, 0)
        eights = total // 8
        lax.fori_loop(0, eights, several(base, 8), 0)
        lax.fori_loop(0, (total - 8 * eights + 1) // 2, several(base + 8 * eights, 2), 0)

    for copy in copies[2:]:
        copy.wait()
    row_deltas(range(count))
    sweep(jnp.int32(0), total)

    parts, part_rows = dk_ref.shape[0], dk_ref.shape[1]
    per = BLK // part_rows
    for j in range(parts):
        dest = pb_me ^ j
        at = pl.multiple_of((dest % per) * part_rows, part_rows)
        dk_ref[j] = dk_acc[dest // per, pl.ds(at, part_rows)] * factor
        dv_ref[j] = dv_acc[dest // per, pl.ds(at, part_rows)]


def backward(lists, lse, queries, outputs, grads, keys, values, sizes):
    ctx_size, pb_size = sizes
    count, rows, width = queries.shape
    grad = pltpu.VMEM((pb_size, BLK_DEV * BLK // pb_size, width), jnp.float32)
    f32, bf16 = jnp.float32, jnp.bfloat16
    own_rows = pltpu.VMEM((count, rows, width), bf16)
    block = pltpu.VMEM((BLK_DEV + 1, BLK, width), bf16)
    row = pltpu.VMEM((count, 1, rows), f32)
    acc = pltpu.VMEM((BLK_DEV + 1, BLK, width), f32)
    slot = pltpu.VMEM((2 * BLK, rows), bf16)
    in_hbm = [pltpu.with_memory_space_constraint(a, pltpu.HBM) for a in (lists, lse, queries, outputs, grads, keys, values)]
    return pl.pallas_call(
        partial(backward_kernel, width ** (-0.5)),
        in_specs=[pl.BlockSpec(memory_space=pltpu.HBM)] * 7,
        out_specs=[pl.BlockSpec(memory_space=pltpu.VMEM)] * 3,
        out_shape=[pltpu.VMEM((ctx_size, count, rows // ctx_size, width), f32), grad, grad],
        scratch_shapes=[own_rows] * 3
        + [block, block, row, row, acc, acc]
        + [slot] * 4
        + [
            pltpu.VMEM(lse.shape, f32),
            pltpu.SMEM(lists.shape, jnp.int32),
            pltpu.SMEM((3, (count + 1) * PAIRS), jnp.int32),
            pltpu.SemaphoreType.DMA((7,)),
        ],
        compiler_params=pltpu.CompilerParams(vmem_limit_bytes=24 * 1024 * 1024),
        cost_estimate=pl.CostEstimate(
            flops=count * rows * BLK_DEV * BLK * width * 10, bytes_accessed=count * rows * width * 12, transcendentals=0
        ),
        name="attention_backward",
    )(*in_hbm)


def swap(array, axis, size, bit):
    return lax.ppermute(array, axis, [(i, i ^ bit) for i in range(size)])


def exchange(groups, axis, size, bit):
    sent = jnp.stack([parts[j] for parts in groups for j in sorted(parts) if j & bit])
    got = iter(swap(sent, axis, size, bit))
    return [{j: parts[j] + next(got) for j in sorted(parts) if not j & bit} for parts in groups]


def bits_of(size):
    return [1 << i for i in range(size.bit_length() - 1)]


def sum_two_ways(first, second, axis, size):
    order = bits_of(size)
    other = order[1::-1] + order[2:]
    for one, two in zip(order, other):
        if one == two:
            first, second = exchange([first, second], axis, size, one)
        else:
            (first,) = exchange([first], axis, size, one)
            (second,) = exchange([second], axis, size, two)
    return first[0], second[0]


def in_one_piece(function, *operands):
    shapes = jax.eval_shape(function, *operands)
    zeros = lambda *_: jax.tree.map(lambda s: jnp.zeros(s.shape, s.dtype), shapes)
    return lax.cond(lax.optimization_barrier(jnp.int32(1)) > 0, function, zeros, *operands)


def local(ctx_size, pb_size, queries, keys, values, outputs_saved, grad_out, saved_lse, block_lists):
    questions, tokens, heads, width = queries.shape
    rows = tokens * heads
    flat = lambda a: a.reshape(questions, rows, width)
    blocked = lambda a: a.reshape(BLK_DEV, BLK, width)
    dq, dk, dv = backward(
        block_lists,
        jnp.swapaxes(saved_lse, 1, 2),
        flat(queries),
        flat(outputs_saved),
        flat(grad_out),
        blocked(keys),
        blocked(values),
        (ctx_size, pb_size),
    )
    far = [j for j in range(2, ctx_size, 2)]
    got = swap(jnp.stack([dq[j | CORE] for j in far]), "ctx", ctx_size, CORE)
    parts = {j: dq[j] + got[n] for n, j in enumerate(far)}
    own, near, dk, dv, parts = lax.optimization_barrier((dq[0], dq[CORE], dk, dv, parts))
    arrived = []
    for bit in bits_of(ctx_size)[1:]:
        sent = [j for j in sorted(parts) if j & bit]
        got = dict(zip(sent, swap(jnp.stack([parts[j] for j in sent]), "ctx", ctx_size, bit)))
        arrived.append(got.pop(bit))
        parts = {j: parts[j] + got[j | bit] for j in parts if not j & bit}
    own = lax.optimization_barrier(own + swap(near, "ctx", ctx_size, CORE))
    by_dest = lambda a: {j: a[j] for j in range(pb_size)}
    sums = partial(sum_two_ways, axis="pb", size=pb_size)
    key_grad, value_grad = in_one_piece(sums, by_dest(dk), by_dest(dv))
    query_grad = sum(arrived, own)
    return query_grad.reshape(questions, tokens // ctx_size, heads, width), key_grad, value_grad


def solution(mesh):
    ctx_size, pb_size = mesh.shape["ctx"], mesh.shape["pb"]
    placed = (
        P("pb", None, None, None),
        P("ctx", None),
        P("ctx", None),
        P("pb", None, None, None),
        P("pb", None, None, None),
        P("pb", None, None),
        P("pb", None),
    )
    return jax.shard_map(
        partial(local, ctx_size, pb_size),
        mesh=mesh,
        in_specs=placed,
        out_specs=(P("pb", "ctx", None, None), P(("ctx", "pb"), None), P(("ctx", "pb"), None)),
        check_vma=False,
    )
```

```python
from functools import partial
import math

import jax
import jax.numpy as jnp
from jax import lax
from jax.experimental import pallas as pl
from jax.experimental.pallas import tpu as pltpu
from jax.sharding import PartitionSpec as P

BLK = 128
BLK_DEV = 8
PAIRS = BLK_DEV // 2
NONE = BLK_DEV
CORE = 1

NN = (((1,), (0,)), ((), ()))
NT = (((1,), (1,)), ((), ()))
TN = (((0,), (0,)), ((), ()))


def mm(a, b, dims):
    return lax.dot_general(a, b, dims, preferred_element_type=jnp.float32)


def list_items(lists, items, questions, base):
    first_block = lax.axis_index("ctx") * BLK_DEV
    below, above = first_block.astype(jnp.uint32), (first_block + BLK_DEV).astype(jnp.uint32)
    last = lists.shape[1] - 1
    end = base
    for i in questions:
        start = jnp.int32(0)
        stop = jnp.int32(0)
        for entry in range(last + 1):
            block = lists[i, entry].astype(jnp.uint32)
            start += (block < below).astype(jnp.int32)
            stop += (block < above).astype(jnp.int32)
        for p in range(PAIRS):
            at = start + 2 * p
            items[0, end + p] = i
            items[1, end + p] = lists[i, jnp.minimum(at, last)] - first_block
            items[2, end + p] = jnp.where(at + 1 < stop, lists[i, jnp.minimum(at + 1, last)] - first_block, NONE)
        end += (stop - start + 1) // 2
    for p in range(2):
        items[0, end + p] = questions[0]
        items[1, end + p] = NONE
        items[2, end + p] = NONE
    return end


def spread_lse(lse, out, rows):
    count, heads, tokens = lse.shape
    rest = lse[...].reshape(count * heads, tokens) * math.log2(math.e)
    row = lax.broadcasted_iota(jnp.int32, (tokens, rows), 1) // heads
    spread = (row == lax.broadcasted_iota(jnp.int32, (tokens, rows), 0)).astype(jnp.bfloat16)
    wide = jnp.zeros((count * heads, rows), jnp.float32)
    for _ in range(3):
        piece = rest.astype(jnp.bfloat16)
        rest = rest - piece.astype(jnp.float32)
        wide += mm(piece, spread, NN)
    head_of_row = lax.broadcasted_iota(jnp.int32, (heads, rows), 1) % heads
    own_head = head_of_row == lax.broadcasted_iota(jnp.int32, (heads, rows), 0)
    for i in range(count):
        picked = jnp.where(own_head, wide[i * heads : (i + 1) * heads], 0.0)
        out[i] = jnp.sum(picked, axis=0, keepdims=True)


def backward_kernel(
    factor,
    lists_hbm, lse_hbm, q_hbm, o_hbm, do_hbm, k_hbm, v_hbm,
    dq_ref, dk_ref, dv_ref,
    q_all, o_all, do_all, k_all, v_all, lse_all, delta_all, dk_acc, dv_acc,
    prob0, prob1, ds0, ds1, lse, lists, items, sems,
):
    prob_slots, ds_slots = (prob0, prob1), (ds0, ds1)
    count, rows, width = q_all.shape
    ctx_me, pb_me = lax.axis_index("ctx"), lax.axis_index("pb")
    copies = [
        pltpu.make_async_copy(src, dst, sems.at[n])
        for n, (src, dst) in enumerate(
            [(lists_hbm, lists), (lse_hbm, lse), (do_hbm, do_all), (o_hbm, o_all), (q_hbm, q_all)]
            + [(src, dst.at[pl.ds(0, BLK_DEV)]) for src, dst in ((k_hbm, k_all), (v_hbm, v_all))]
        )
    ]
    for copy in copies:
        copy.start()

    dq_ref[...] = jnp.zeros_like(dq_ref)
    dk_acc[...] = jnp.zeros_like(dk_acc)
    dv_acc[...] = jnp.zeros_like(dv_acc)
    k_all[NONE] = jnp.zeros((BLK, width), k_all.dtype)
    v_all[NONE] = jnp.zeros((BLK, width), v_all.dtype)
    copies[0].wait()
    total = list_items(lists, items, range(count), jnp.int32(0))
    copies[1].wait()
    spread_lse(lse, lse_all, rows)
    scale = factor * math.log2(math.e)
    parts, part_rows = dq_ref.shape[0], dq_ref.shape[2]

    def row_deltas(questions):
        ones = jnp.ones((8, 2 * width), jnp.bfloat16)
        for i in questions:
            product = do_all[i].astype(jnp.float32) * o_all[i].astype(jnp.float32)
            high = product.astype(jnp.bfloat16)
            low = (product - high.astype(jnp.float32)).astype(jnp.bfloat16)
            delta_all[i] = mm(ones, jnp.concatenate([high, low], axis=1), NT)[0:1]

    def scores(item, slot):
        i, b0, b1 = items[0, item], items[1, item], items[2, item]
        keys = jnp.concatenate([k_all[b0], k_all[b1]], axis=0)
        values = jnp.concatenate([v_all[b0], v_all[b1]], axis=0)
        prob = jnp.exp2(mm(keys, q_all[i], NT) * scale - lse_all[i])
        dprob = mm(values, do_all[i], NT)
        prob_slots[slot][...] = prob.astype(jnp.bfloat16)
        ds_slots[slot][...] = (prob * (dprob - delta_all[i])).astype(jnp.bfloat16)

    def gradients(item, slot):
        i, b0, b1 = items[0, item], items[1, item], items[2, item]
        keys = jnp.concatenate([k_all[b0], k_all[b1]], axis=0)
        dscore = ds_slots[slot][...]
        dv = mm(prob_slots[slot][...], do_all[i], NN)
        dk = mm(dscore, q_all[i], NN)
        dq = mm(dscore, keys, TN) * factor
        for j in range(parts):
            dq_ref[ctx_me ^ j, i] += dq[j * part_rows : (j + 1) * part_rows]
        dv_acc[b0] += dv[:BLK]
        dk_acc[b0] += dk[:BLK]
        dv_acc[b1] += dv[BLK:]
        dk_acc[b1] += dk[BLK:]

    def sweep(base, total):
        def several(first, step_items):
            def body(step, carry):
                at = first + step_items * step
                for n in range(0, step_items, 2):
                    scores(at + n + 1, 1)
                    gradients(at + n, 0)
                    scores(at + n + 2, 0)
                    gradients(at + n + 1, 1)
                return carry

            return body

        scores(base, 0)
        eights = total // 8
        lax.fori_loop(0, eights, several(base, 8), 0)
        lax.fori_loop(0, (total - 8 * eights + 1) // 2, several(base + 8 * eights, 2), 0)

    for copy in copies[2:]:
        copy.wait()
    row_deltas(range(count))
    sweep(jnp.int32(0), total)

    parts, part_rows = dk_ref.shape[0], dk_ref.shape[1]
    per = BLK // part_rows
    for j in range(parts):
        dest = pb_me ^ j
        at = pl.multiple_of((dest % per) * part_rows, part_rows)
        dk_ref[j] = dk_acc[dest // per, pl.ds(at, part_rows)] * factor
        dv_ref[j] = dv_acc[dest // per, pl.ds(at, part_rows)]


def backward(lists, lse, queries, outputs, grads, keys, values, sizes):
    ctx_size, pb_size = sizes
    count, rows, width = queries.shape
    grad = pltpu.VMEM((pb_size, BLK_DEV * BLK // pb_size, width), jnp.float32)
    f32, bf16 = jnp.float32, jnp.bfloat16
    own_rows = pltpu.VMEM((count, rows, width), bf16)
    block = pltpu.VMEM((BLK_DEV + 1, BLK, width), bf16)
    row = pltpu.VMEM((count, 1, rows), f32)
    acc = pltpu.VMEM((BLK_DEV + 1, BLK, width), f32)
    slot = pltpu.VMEM((2 * BLK, rows), bf16)
    in_hbm = [pltpu.with_memory_space_constraint(a, pltpu.HBM) for a in (lists, lse, queries, outputs, grads, keys, values)]
    return pl.pallas_call(
        partial(backward_kernel, width ** (-0.5)),
        in_specs=[pl.BlockSpec(memory_space=pltpu.HBM)] * 7,
        out_specs=[pl.BlockSpec(memory_space=pltpu.VMEM)] * 3,
        out_shape=[pltpu.VMEM((ctx_size, count, rows // ctx_size, width), f32), grad, grad],
        scratch_shapes=[own_rows] * 3
        + [block, block, row, row, acc, acc]
        + [slot] * 4
        + [
            pltpu.VMEM(lse.shape, f32),
            pltpu.SMEM(lists.shape, jnp.int32),
            pltpu.SMEM((3, (count + 1) * PAIRS), jnp.int32),
            pltpu.SemaphoreType.DMA((7,)),
        ],
        compiler_params=pltpu.CompilerParams(vmem_limit_bytes=24 * 1024 * 1024),
        cost_estimate=pl.CostEstimate(
            flops=count * rows * BLK_DEV * BLK * width * 10, bytes_accessed=count * rows * width * 12, transcendentals=0
        ),
        name="attention_backward",
    )(*in_hbm)


def sum_kernel(cuts, *refs):
    ins, out, slots, sems = refs[: len(refs) // 2 - 1], refs[len(refs) // 2 - 1], refs[len(refs) // 2 : -1], refs[-1]
    rows = out.shape[0] // cuts
    cut = lambda ref, n: ref.at[pl.ds(n * rows, rows)]
    loads = [
        [pltpu.make_async_copy(cut(src, n), cut(dst, n), sems.at[m, n]) for m, (src, dst) in enumerate(zip(ins, slots))]
        for n in range(cuts)
    ]
    stores = [pltpu.make_async_copy(cut(slots[-1], n), cut(out, n), sems.at[len(ins), n]) for n in range(cuts)]
    for load in loads:
        for copy in load:
            copy.start()
    for n, load in enumerate(loads):
        for copy in load:
            copy.wait()
        total = cut(slots[0], n)[...]
        for slot in slots[1:-1]:
            total += cut(slot, n)[...]
        cut(slots[-1], n)[...] = total
        stores[n].start()
    for store in stores:
        store.wait()


def sum_in_hbm(arrays, cuts=4):
    like, n = arrays[0], len(arrays)
    return pl.pallas_call(
        partial(sum_kernel, cuts),
        in_specs=[pl.BlockSpec(memory_space=pl.ANY)] * n,
        out_specs=pl.BlockSpec(memory_space=pltpu.HBM),
        out_shape=pltpu.HBM(like.shape, like.dtype),
        scratch_shapes=[pltpu.VMEM(like.shape, like.dtype)] * (n + 1) + [pltpu.SemaphoreType.DMA((n + 1, cuts))],
        compiler_params=pltpu.CompilerParams(vmem_limit_bytes=12 * 1024 * 1024),
        name="sum_parts",
    )(*arrays)


def swap(array, axis, size, bit):
    return lax.ppermute(array, axis, [(i, i ^ bit) for i in range(size)])


def exchange(groups, axis, size, bit):
    sent = jnp.stack([parts[j] for parts in groups for j in sorted(parts) if j & bit])
    got = iter(swap(sent, axis, size, bit))
    return [{j: parts[j] + next(got) for j in sorted(parts) if not j & bit} for parts in groups]


def bits_of(size):
    return [1 << i for i in range(size.bit_length() - 1)]


def sum_two_ways(first, second, axis, size):
    order = bits_of(size)
    other = order[1::-1] + order[2:]
    for one, two in zip(order, other):
        if one == two:
            first, second = exchange([first, second], axis, size, one)
        else:
            (first,) = exchange([first], axis, size, one)
            (second,) = exchange([second], axis, size, two)
    return first[0], second[0]


def in_one_piece(function, *operands):
    shapes = jax.eval_shape(function, *operands)
    zeros = lambda *_: jax.tree.map(lambda s: jnp.zeros(s.shape, s.dtype), shapes)
    return lax.cond(lax.optimization_barrier(jnp.int32(1)) > 0, function, zeros, *operands)


def local(ctx_size, pb_size, queries, keys, values, outputs_saved, grad_out, saved_lse, block_lists):
    questions, tokens, heads, width = queries.shape
    rows = tokens * heads
    flat = lambda a: a.reshape(questions, rows, width)
    blocked = lambda a: a.reshape(BLK_DEV, BLK, width)
    dq, dk, dv = backward(
        block_lists,
        jnp.swapaxes(saved_lse, 1, 2),
        flat(queries),
        flat(outputs_saved),
        flat(grad_out),
        blocked(keys),
        blocked(values),
        (ctx_size, pb_size),
    )
    far = [j for j in range(2, ctx_size, 2)]
    got = swap(jnp.stack([dq[j | CORE] for j in far]), "ctx", ctx_size, CORE)
    parts = {j: dq[j] + got[n] for n, j in enumerate(far)}
    own, near, dk, dv, parts = lax.optimization_barrier((dq[0], dq[CORE], dk, dv, parts))
    arrived = []
    for bit in bits_of(ctx_size)[1:]:
        sent = [j for j in sorted(parts) if j & bit]
        got = dict(zip(sent, swap(jnp.stack([parts[j] for j in sent]), "ctx", ctx_size, bit)))
        arrived.append(got.pop(bit))
        parts = {j: parts[j] + got[j | bit] for j in parts if not j & bit}
    own = lax.optimization_barrier(own + swap(near, "ctx", ctx_size, CORE))
    by_dest = lambda a: {j: a[j] for j in range(pb_size)}
    sums = partial(sum_two_ways, axis="pb", size=pb_size)
    key_grad, value_grad = in_one_piece(sums, by_dest(dk), by_dest(dv))
    query_grad = sum_in_hbm([own] + arrived)
    return query_grad.reshape(questions, tokens // ctx_size, heads, width), key_grad, value_grad


def solution(mesh):
    ctx_size, pb_size = mesh.shape["ctx"], mesh.shape["pb"]
    placed = (
        P("pb", None, None, None),
        P("ctx", None),
        P("ctx", None),
        P("pb", None, None, None),
        P("pb", None, None, None),
        P("pb", None, None),
        P("pb", None),
    )
    return jax.shard_map(
        partial(local, ctx_size, pb_size),
        mesh=mesh,
        in_specs=placed,
        out_specs=(P("pb", "ctx", None, None), P(("ctx", "pb"), None), P(("ctx", "pb"), None)),
        check_vma=False,
    )
```

```python
from functools import partial
import math

import jax
import jax.numpy as jnp
from jax import lax
from jax.experimental import pallas as pl
from jax.experimental.pallas import tpu as pltpu
from jax.sharding import PartitionSpec as P

BLK = 128
BLK_DEV = 8
PAIRS = BLK_DEV // 2
NONE = BLK_DEV
CORE = 1

NN = (((1,), (0,)), ((), ()))
NT = (((1,), (1,)), ((), ()))
TN = (((0,), (0,)), ((), ()))


def mm(a, b, dims):
    return lax.dot_general(a, b, dims, preferred_element_type=jnp.float32)


def list_items(lists, items, questions, base):
    first_block = lax.axis_index("ctx") * BLK_DEV
    below, above = first_block.astype(jnp.uint32), (first_block + BLK_DEV).astype(jnp.uint32)
    last = lists.shape[1] - 1
    end = base
    for i in questions:
        start = jnp.int32(0)
        stop = jnp.int32(0)
        for entry in range(last + 1):
            block = lists[i, entry].astype(jnp.uint32)
            start += (block < below).astype(jnp.int32)
            stop += (block < above).astype(jnp.int32)
        for p in range(PAIRS):
            at = start + 2 * p
            items[0, end + p] = i
            items[1, end + p] = lists[i, jnp.minimum(at, last)] - first_block
            items[2, end + p] = jnp.where(at + 1 < stop, lists[i, jnp.minimum(at + 1, last)] - first_block, NONE)
        end += (stop - start + 1) // 2
    for p in range(2):
        items[0, end + p] = questions[0]
        items[1, end + p] = NONE
        items[2, end + p] = NONE
    return end


def spread_lse(lse, out, rows):
    count, heads, tokens = lse.shape
    rest = lse[...].reshape(count * heads, tokens) * math.log2(math.e)
    row = lax.broadcasted_iota(jnp.int32, (tokens, rows), 1) // heads
    spread = (row == lax.broadcasted_iota(jnp.int32, (tokens, rows), 0)).astype(jnp.bfloat16)
    wide = jnp.zeros((count * heads, rows), jnp.float32)
    for _ in range(3):
        piece = rest.astype(jnp.bfloat16)
        rest = rest - piece.astype(jnp.float32)
        wide += mm(piece, spread, NN)
    head_of_row = lax.broadcasted_iota(jnp.int32, (heads, rows), 1) % heads
    own_head = head_of_row == lax.broadcasted_iota(jnp.int32, (heads, rows), 0)
    for i in range(count):
        picked = jnp.where(own_head, wide[i * heads : (i + 1) * heads], 0.0)
        out[i] = jnp.sum(picked, axis=0, keepdims=True)


def backward_kernel(
    factor,
    lists_hbm, lse_hbm, q_hbm, o_hbm, do_hbm, k_hbm, v_hbm,
    dq_ref, dk_ref, dv_ref,
    q_all, o_all, do_all, k_all, v_all, lse_all, delta_all, dk_acc, dv_acc,
    prob0, prob1, ds0, ds1, lse, lists, items, sems,
):
    prob_slots, ds_slots = (prob0, prob1), (ds0, ds1)
    count, rows, width = q_all.shape
    ctx_me, pb_me = lax.axis_index("ctx"), lax.axis_index("pb")
    copies = [
        pltpu.make_async_copy(src, dst, sems.at[n])
        for n, (src, dst) in enumerate(
            [(lists_hbm, lists), (lse_hbm, lse), (do_hbm, do_all), (o_hbm, o_all), (q_hbm, q_all)]
            + [(src, dst.at[pl.ds(0, BLK_DEV)]) for src, dst in ((k_hbm, k_all), (v_hbm, v_all))]
        )
    ]
    for copy in copies:
        copy.start()

    dq_ref[...] = jnp.zeros_like(dq_ref)
    dk_acc[...] = jnp.zeros_like(dk_acc)
    dv_acc[...] = jnp.zeros_like(dv_acc)
    k_all[NONE] = jnp.zeros((BLK, width), k_all.dtype)
    v_all[NONE] = jnp.zeros((BLK, width), v_all.dtype)
    copies[0].wait()
    total = list_items(lists, items, range(count), jnp.int32(0))
    copies[1].wait()
    spread_lse(lse, lse_all, rows)
    scale = factor * math.log2(math.e)
    parts, part_rows = dq_ref.shape[0], dq_ref.shape[2]

    def row_deltas(questions):
        ones = jnp.ones((8, 2 * width), jnp.bfloat16)
        for i in questions:
            product = do_all[i].astype(jnp.float32) * o_all[i].astype(jnp.float32)
            high = product.astype(jnp.bfloat16)
            low = (product - high.astype(jnp.float32)).astype(jnp.bfloat16)
            delta_all[i] = mm(ones, jnp.concatenate([high, low], axis=1), NT)[0:1]

    def scores(item, slot):
        i, b0, b1 = items[0, item], items[1, item], items[2, item]
        keys = jnp.concatenate([k_all[b0], k_all[b1]], axis=0)
        values = jnp.concatenate([v_all[b0], v_all[b1]], axis=0)
        prob = jnp.exp2(mm(keys, q_all[i], NT) * scale - lse_all[i])
        dprob = mm(values, do_all[i], NT)
        prob_slots[slot][...] = prob.astype(jnp.bfloat16)
        ds_slots[slot][...] = (prob * (dprob - delta_all[i])).astype(jnp.bfloat16)

    def gradients(item, slot):
        i, b0, b1 = items[0, item], items[1, item], items[2, item]
        keys = jnp.concatenate([k_all[b0], k_all[b1]], axis=0)
        dscore = ds_slots[slot][...]
        dv = mm(prob_slots[slot][...], do_all[i], NN)
        dk = mm(dscore, q_all[i], NN)
        dq = mm(dscore, keys, TN) * factor
        for j in range(parts):
            dq_ref[ctx_me ^ j, i] += dq[j * part_rows : (j + 1) * part_rows]
        dv_acc[b0] += dv[:BLK]
        dk_acc[b0] += dk[:BLK]
        dv_acc[b1] += dv[BLK:]
        dk_acc[b1] += dk[BLK:]

    def sweep(base, total):
        def several(first, step_items):
            def body(step, carry):
                at = first + step_items * step
                for n in range(0, step_items, 2):
                    scores(at + n + 1, 1)
                    gradients(at + n, 0)
                    scores(at + n + 2, 0)
                    gradients(at + n + 1, 1)
                return carry

            return body

        scores(base, 0)
        eights = total // 8
        lax.fori_loop(0, eights, several(base, 8), 0)
        lax.fori_loop(0, (total - 8 * eights + 1) // 2, several(base + 8 * eights, 2), 0)

    for copy in copies[2:]:
        copy.wait()
    row_deltas(range(count))
    sweep(jnp.int32(0), total)

    parts, part_rows = dk_ref.shape[0], dk_ref.shape[1]
    per = BLK // part_rows
    for j in range(parts):
        dest = pb_me ^ j
        at = pl.multiple_of((dest % per) * part_rows, part_rows)
        dk_ref[j] = dk_acc[dest // per, pl.ds(at, part_rows)] * factor
        dv_ref[j] = dv_acc[dest // per, pl.ds(at, part_rows)]


def backward(lists, lse, queries, outputs, grads, keys, values, sizes):
    ctx_size, pb_size = sizes
    count, rows, width = queries.shape
    grad = pltpu.VMEM((pb_size, BLK_DEV * BLK // pb_size, width), jnp.float32)
    f32, bf16 = jnp.float32, jnp.bfloat16
    own_rows = pltpu.VMEM((count, rows, width), bf16)
    block = pltpu.VMEM((BLK_DEV + 1, BLK, width), bf16)
    row = pltpu.VMEM((count, 1, rows), f32)
    acc = pltpu.VMEM((BLK_DEV + 1, BLK, width), f32)
    slot = pltpu.VMEM((2 * BLK, rows), bf16)
    in_hbm = [pltpu.with_memory_space_constraint(a, pltpu.HBM) for a in (lists, lse, queries, outputs, grads, keys, values)]
    return pl.pallas_call(
        partial(backward_kernel, width ** (-0.5)),
        in_specs=[pl.BlockSpec(memory_space=pltpu.HBM)] * 7,
        out_specs=[pl.BlockSpec(memory_space=pltpu.VMEM)] * 3,
        out_shape=[pltpu.VMEM((ctx_size, count, rows // ctx_size, width), f32), grad, grad],
        scratch_shapes=[own_rows] * 3
        + [block, block, row, row, acc, acc]
        + [slot] * 4
        + [
            pltpu.VMEM(lse.shape, f32),
            pltpu.SMEM(lists.shape, jnp.int32),
            pltpu.SMEM((3, (count + 1) * PAIRS), jnp.int32),
            pltpu.SemaphoreType.DMA((7,)),
        ],
        compiler_params=pltpu.CompilerParams(vmem_limit_bytes=24 * 1024 * 1024),
        cost_estimate=pl.CostEstimate(
            flops=count * rows * BLK_DEV * BLK * width * 10, bytes_accessed=count * rows * width * 12, transcendentals=0
        ),
        name="attention_backward",
    )(*in_hbm)


def sum_kernel(cuts, *refs):
    ins, out, slots, sems = refs[: len(refs) // 2 - 1], refs[len(refs) // 2 - 1], refs[len(refs) // 2 : -1], refs[-1]
    rows = out.shape[0] // cuts
    cut = lambda ref, n: ref.at[pl.ds(n * rows, rows)]
    loads = [
        [pltpu.make_async_copy(cut(src, n), cut(dst, n), sems.at[m, n]) for m, (src, dst) in enumerate(zip(ins, slots))]
        for n in range(cuts)
    ]
    stores = [pltpu.make_async_copy(cut(slots[-1], n), cut(out, n), sems.at[len(ins), n]) for n in range(cuts)]
    for load in loads:
        for copy in load:
            copy.start()
    for n, load in enumerate(loads):
        for copy in load:
            copy.wait()
        total = cut(slots[0], n)[...]
        for slot in slots[1:-1]:
            total += cut(slot, n)[...]
        cut(slots[-1], n)[...] = total
        stores[n].start()
    for store in stores:
        store.wait()


def sum_in_hbm(arrays, cuts=4):
    like, n = arrays[0], len(arrays)
    return pl.pallas_call(
        partial(sum_kernel, cuts),
        in_specs=[pl.BlockSpec(memory_space=pl.ANY)] * n,
        out_specs=pl.BlockSpec(memory_space=pltpu.HBM),
        out_shape=pltpu.HBM(like.shape, like.dtype),
        scratch_shapes=[pltpu.VMEM(like.shape, like.dtype)] * (n + 1) + [pltpu.SemaphoreType.DMA((n + 1, cuts))],
        compiler_params=pltpu.CompilerParams(vmem_limit_bytes=12 * 1024 * 1024),
        name="sum_parts",
    )(*arrays)


def swap(array, axis, size, bit):
    return lax.ppermute(array, axis, [(i, i ^ bit) for i in range(size)])


def exchange(groups, axis, size, bit):
    sent = jnp.stack([parts[j] for parts in groups for j in sorted(parts) if j & bit])
    got = iter(swap(sent, axis, size, bit))
    return [{j: parts[j] + next(got) for j in sorted(parts) if not j & bit} for parts in groups]


def bits_of(size):
    return [1 << i for i in range(size.bit_length() - 1)]


def sum_two_ways(first, second, axis, size):
    order = bits_of(size)
    other = order[1::-1] + order[2:]
    for one, two in zip(order, other):
        if one == two:
            first, second = exchange([first, second], axis, size, one)
        else:
            (first,) = exchange([first], axis, size, one)
            (second,) = exchange([second], axis, size, two)
    return first[0], second[0]


def in_one_piece(function, *operands):
    shapes = jax.eval_shape(function, *operands)
    zeros = lambda *_: jax.tree.map(lambda s: jnp.zeros(s.shape, s.dtype), shapes)
    return lax.cond(lax.optimization_barrier(jnp.int32(1)) > 0, function, zeros, *operands)


def local(ctx_size, pb_size, queries, keys, values, outputs_saved, grad_out, saved_lse, block_lists):
    questions, tokens, heads, width = queries.shape
    rows = tokens * heads
    flat = lambda a: a.reshape(questions, rows, width)
    blocked = lambda a: a.reshape(BLK_DEV, BLK, width)
    dq, dk, dv = backward(
        block_lists,
        jnp.swapaxes(saved_lse, 1, 2),
        flat(queries),
        flat(outputs_saved),
        flat(grad_out),
        blocked(keys),
        blocked(values),
        (ctx_size, pb_size),
    )
    far = [j for j in range(2, ctx_size, 2)]
    got = swap(jnp.stack([dq[j | CORE] for j in far]), "ctx", ctx_size, CORE)
    parts = {j: dq[j] + got[n] for n, j in enumerate(far)}
    near, dk, dv, parts = lax.optimization_barrier((dq[CORE], dk, dv, parts))
    arrived = []
    for bit in bits_of(ctx_size)[1:]:
        sent = [j for j in sorted(parts) if j & bit]
        got = dict(zip(sent, swap(jnp.stack([parts[j] for j in sent]), "ctx", ctx_size, bit)))
        arrived.append(got.pop(bit))
        parts = {j: parts[j] + got[j | bit] for j in parts if not j & bit}
    near = swap(near, "ctx", ctx_size, CORE)
    by_dest = lambda a: {j: a[j] for j in range(pb_size)}

    def sums(dk, dv, own, near):
        return *sum_two_ways(by_dest(dk), by_dest(dv), "pb", pb_size), own[0] + near

    key_grad, value_grad, own = in_one_piece(sums, dk, dv, dq, near)
    query_grad = sum_in_hbm([own] + arrived)
    return query_grad.reshape(questions, tokens // ctx_size, heads, width), key_grad, value_grad


def solution(mesh):
    ctx_size, pb_size = mesh.shape["ctx"], mesh.shape["pb"]
    placed = (
        P("pb", None, None, None),
        P("ctx", None),
        P("ctx", None),
        P("pb", None, None, None),
        P("pb", None, None, None),
        P("pb", None, None),
        P("pb", None),
    )
    return jax.shard_map(
        partial(local, ctx_size, pb_size),
        mesh=mesh,
        in_specs=placed,
        out_specs=(P("pb", "ctx", None, None), P(("ctx", "pb"), None), P(("ctx", "pb"), None)),
        check_vma=False,
    )
```
